32 devices in a mesh: snp: 8 (over y, x, core), prog: 4 (over z).
Axes of the slice: x: 2, y: 2, z: 4, core: 2. Of those that a mesh axis runs over, the one named last changes fastest.
Arguments:
- gene_score: bfloat16 [1024, 1024], P('snp', 'prog'), may hold values from 0 to 1
- link_gene: int32 [24576, 8], P('snp'), may hold values from 0 to 1023, as said below
- link_weight: bfloat16 [24576, 8], P('snp'), may hold values from 0.099609375 to 1
- ld_levels: bfloat16 [192, 5, 128, 128], P('snp'), may hold values from 0 to 1
- ld_scale: float32 [192, 5], P('snp'), may hold values from 0.2 to 1
- snp_weight: float32 [24576], P('snp'), may hold values from 0.25 to 6, as said below
- trait_z: bfloat16 [24576, 4096], P('snp', 'prog'), may hold values from -6 to 6
- jk_unit: int32 [8, 12], P('snp'), may hold values from 0 to 2, never falling along the last dimension, each value on 1 to 6 neighbouring positions
Outputs:
- delete_one: bfloat16 [24, 1024, 4096], P('snp', None, 'prog')
- block_estimate: bfloat16 [24, 1024, 4096], P('snp', None, 'prog')
The draws below stay inside these ranges and needn't reach their ends.
Inputs may be any that keep to these rules, and one draw needn't show every extreme that they name: `link_gene`: A SNP of slab i names 8 distinct genes, all in gene blocks i - 1, i and i + 1 (block b holds genes b * 128 to (b + 1) * 128 - 1; blocks before the first and after the last don't exist). `snp_weight`: Positive. `jk_unit`: along each row the numbers never fall and each of the 3 numbers appears; a block holds at most 6 units, and some block of each row exactly that many.
All inputs are finite; a program needn't handle non-finite values.
Results may differ from the reference program's by a relative error of at most 0.012.
Values may be sent and summed in bfloat16 or wider, within the bound.
A program may use at most 192 MiB of HBM per device.

```python
import math
import jax
import jax.numpy as jnp
import numpy as np
from jax import lax

P_SIZE = 1024
K = 4096
SNP_DEV = 3072
GENE_DEV = 128
LINKS = 8
B = 128
W = 2
UNIT = 256
JK_DEV = 3
SNPS = 24576
NB = 192
UNITS_DEV = 12
JK = 24
N_SNP = 8


def draw_link_gene(key, part):
    row_total = SNP_DEV * N_SNP
    row_ids = lax.broadcasted_iota(jnp.int32, (row_total, LINKS), 0)
    slot_ids = lax.broadcasted_iota(jnp.int32, (row_total, LINKS), 1)
    slab = row_ids // SNP_DEV
    wide_step = 3 * GENE_DEV // LINKS
    narrow_step = 2 * GENE_DEV // LINKS
    at_edge = jnp.logical_or(slab == 0, slab == N_SNP - 1)
    step_size = jnp.where(at_edge, narrow_step, wide_step)
    jitter = jax.random.randint(key, (row_total, LINKS), 0, 1 << 20, jnp.int32) % step_size
    offset = slot_ids * step_size + jitter
    first_gene = jnp.where(slab == 0, 0, (slab - 1) * GENE_DEV)
    return (first_gene + offset).astype(jnp.int32)


def draw_snp_weight(key, part):
    row_total = SNP_DEV * N_SNP
    position = lax.broadcasted_iota(jnp.float32, (row_total,), 0) / row_total
    base = jnp.exp(jnp.log(3.0) * position)
    rough = jnp.exp(jax.random.uniform(key, (row_total,), jnp.float32, jnp.log(0.5), jnp.log(2.0)))
    return (base * rough).astype(jnp.float32)


def draw_gene_score(key, part):
    gene_total = GENE_DEV * N_SNP
    scale_key = jax.random.fold_in(key, 11)
    keep_key = jax.random.fold_in(key, 12)
    value_key = jax.random.fold_in(key, 13)
    keep = jax.random.randint(keep_key, (gene_total, P_SIZE), 0, 2, jnp.int32) == 0
    row_scale = jnp.exp(jax.random.uniform(scale_key, (gene_total, 1), jnp.float32, jnp.log(0.1), 0.0))
    value = jax.random.uniform(value_key, (gene_total, P_SIZE), jnp.float32, 0.0, 1.0)
    return jnp.where(keep, row_scale * value, 0.0).astype(jnp.bfloat16)


def draw_ld_levels(key, part):
    band = 2 * W + 1
    tile_total = SNP_DEV * N_SNP // B
    offset = lax.broadcasted_iota(jnp.int32, (1, band, B, B), 1)
    row_pos = lax.broadcasted_iota(jnp.int32, (1, band, B, B), 2)
    col_pos = lax.broadcasted_iota(jnp.int32, (1, band, B, B), 3)
    distance = (offset - W) * B + col_pos - row_pos
    decay = jnp.exp(-jnp.abs(distance).astype(jnp.float32) / (W * B))
    keep_key = jax.random.fold_in(key, 21)
    value_key = jax.random.fold_in(key, 22)
    keep = jax.random.randint(keep_key, (tile_total, band, B, B), 0, 8, jnp.int32) == 0
    noise = jax.random.uniform(value_key, (tile_total, band, B, B), jnp.float32, 0.0, 1.0)
    levels = jnp.where(keep, decay * noise, 0.0)
    levels = jnp.where(distance == 0, 1.0, levels)
    return levels.astype(jnp.bfloat16)


def block_scale(rng, extent, split, low, high):
    def one(axis_at, parts):
        steps = jax.random.uniform(jax.random.fold_in(jax.random.fold_in(rng, 6), axis_at), (parts,), jnp.float32, low / len(split), high / len(split))
        return jnp.repeat(jnp.exp(steps), extent[axis_at] // parts).reshape((-1,) + (1,) * (len(extent) - axis_at - 1))

    factor_of = one(*split[0])
    for cut in split[1:]:
        factor_of = factor_of * one(*cut)
    return factor_of


def profile(count, total, limit, lean):
    portions = [(1 << 20) // math.isqrt(grade ** lean) + 1 for grade in range(2, count + 1)]
    surplus, counts = total - limit - (count - 1), [1] * (count - 1)
    while surplus > 0:
        free = [i for i in range(count - 1) if counts[i] < limit]
        whole, left = sum([portions[i] for i in free]), surplus
        for i in free:
            more = min(limit - counts[i], max(1, left * portions[i] // whole), surplus)
            counts[i] = counts[i] + more
            surplus = surplus - more
    return np.array([limit] + counts)


def uneven(rng, count, total, reach, skew):
    if count == 2:
        one = jax.random.randint(rng, (), max(1, total - reach), min(reach, total - 1) + 1)
        return jnp.stack([one, total - one])
    sizes = jnp.asarray(profile(count, total, reach, skew), jnp.int32)
    twos = (count - 1) // 2
    giver, receiver = sizes[1:1 + 2 * twos:2], sizes[2:2 + 2 * twos:2]
    room = jnp.minimum(giver - 1, reach - receiver)
    moved = jax.random.randint(jax.random.fold_in(rng, 1), (twos,), 0, 1 << 20) % (room + 1)
    sizes = sizes.at[1:1 + 2 * twos:2].set(giver - moved).at[2:2 + 2 * twos:2].set(receiver + moved)
    return sizes[jax.random.permutation(jax.random.fold_in(rng, 2), count)]


def centred(stream_key, shape, spread, limit, pieces=(), kind=jnp.bfloat16):
    values = spread * jax.random.normal(stream_key, shape, jnp.float32)
    if pieces:
        values = values * block_scale(stream_key, shape, pieces, -0.22, 0.18)
    return jnp.clip(values, -limit, limit).astype(kind)


def setup_inputs(seed: int = 0) -> dict:
    seeds = jax.random.split(jax.random.key(seed), 9)
    return {
        "gene_score": draw_gene_score(jax.random.fold_in(seeds[8], 71), 0),
        "link_gene": draw_link_gene(jax.random.fold_in(seeds[8], 71), 0),
        "link_weight": jnp.clip(jnp.exp(math.log(1.0) - 2.306499 * jax.random.uniform(seeds[2], (SNPS, LINKS), jnp.float32) ** block_scale(seeds[2], (SNPS, LINKS), ((0, 8),), -0.2, 0.2)), 0.099609375, 1.0).astype(jnp.bfloat16),
        "ld_levels": draw_ld_levels(jax.random.fold_in(seeds[8], 71), 0),
        "ld_scale": jnp.clip(jnp.exp(math.log(1.0) - 1.609438 * jax.random.uniform(seeds[4], (NB, 2 * W + 1), jnp.float32) ** block_scale(seeds[4], (NB, 2 * W + 1), ((0, 8),), -0.2, 0.2)), 0.2, 1.0),
        "snp_weight": draw_snp_weight(jax.random.fold_in(seeds[8], 71), 0),
        "trait_z": centred(seeds[6], (SNPS, K), 1.0, 6.0, ((0, 8), (1, 4))),
        "jk_unit": jax.vmap(lambda own: jnp.searchsorted(jnp.cumsum(uneven(own, JK_DEV, UNITS_DEV, UNITS_DEV - 2 - (UNITS_DEV - 3) // 2, 2)), jnp.arange(UNITS_DEV), side="right"))(jax.random.split(seeds[7], N_SNP)).reshape((N_SNP, UNITS_DEV)).astype(jnp.int32),
    }


def reference(gene_score, link_gene, link_weight, ld_levels, ld_scale, snp_weight, trait_z, jk_unit):
    annotation = jnp.zeros((SNPS, P_SIZE), jnp.float32)
    for link_slot in range(LINKS):
        linked = gene_score[link_gene[:, link_slot]].astype(jnp.float32)
        annotation = annotation + link_weight[:, link_slot:link_slot + 1].astype(jnp.float32) * linked
    annotation = annotation.astype(jnp.bfloat16)
    reach_rows = W * B
    padded = jnp.pad(annotation, ((reach_rows, reach_rows), (0, 0)))
    tile_count = SNPS // B
    banded = jnp.zeros((tile_count, B, P_SIZE), jnp.float32)
    for offset in range(2 * W + 1):
        window = padded[offset * B:offset * B + SNPS].reshape(tile_count, B, P_SIZE).astype(jnp.float32)
        levels = ld_levels[:, offset].astype(jnp.float32)
        product = jnp.einsum('nrt,ntp->nrp', levels, window, precision=lax.Precision.HIGHEST)
        banded = banded + ld_scale[:, offset][:, None, None] * product
    ld_score = banded.reshape(SNPS, P_SIZE).astype(jnp.bfloat16)
    ld_float = ld_score.astype(jnp.float32)
    weighted = (snp_weight[:, None] * ld_float).astype(jnp.bfloat16)
    squares = snp_weight[:, None] * ld_float * ld_float

    def slab_terms(slab):
        first_row = slab * SNP_DEV
        slab_weighted = lax.dynamic_slice_in_dim(weighted, first_row, SNP_DEV, 0).astype(jnp.float32)
        slab_traits = lax.dynamic_slice_in_dim(trait_z, first_row, SNP_DEV, 0).astype(jnp.float32)
        slab_squares = lax.dynamic_slice_in_dim(squares, first_row, SNP_DEV, 0)
        per_unit = jnp.einsum('urp,urk->upk', slab_weighted.reshape(UNITS_DEV, UNIT, P_SIZE), slab_traits.reshape(UNITS_DEV, UNIT, K), precision=lax.Precision.HIGHEST)
        unit_squares = slab_squares.reshape(UNITS_DEV, UNIT, P_SIZE).sum(axis=1)
        member = (jk_unit[slab][None, :] == lax.broadcasted_iota(jnp.int32, (JK_DEV, UNITS_DEV), 0)).astype(jnp.float32)
        crossed = jnp.einsum('ju,upk->jpk', member, per_unit, precision=lax.Precision.HIGHEST)
        square_share = jnp.dot(member, unit_squares, precision=lax.Precision.HIGHEST)
        return (crossed, square_share)
    crossed, square_share = lax.map(slab_terms, jnp.arange(N_SNP, dtype=jnp.int32))
    crossed = crossed.reshape(JK, P_SIZE, K)
    square_share = square_share.reshape(JK, P_SIZE)
    summed = lax.optimization_barrier(jnp.sum(crossed, axis=0))
    summed_sq = lax.optimization_barrier(jnp.sum(square_share, axis=0))
    estimate = (summed[None] - crossed) / jnp.sqrt(summed_sq[None] - square_share)[:, :, None]
    own_estimate = crossed / jnp.sqrt(square_share)[:, :, None]
    return (estimate.astype(jnp.bfloat16), own_estimate.astype(jnp.bfloat16))
```

```python
import functools

import jax
import jax.numpy as jnp
from jax import lax
from jax.experimental import pallas as pl
from jax.experimental.pallas import tpu as pltpu
from jax.sharding import PartitionSpec as P

JK_DEV = 3
MESH = pl.DeviceIdType.MESH
F32 = jnp.float32
BF16 = jnp.bfloat16
ROW_CHUNKS = 4


def nt_dot(a, b, **kw):
    return lax.dot_general(a, b, (((1,), (1,)), ((), ())), preferred_element_type=F32, **kw)


def gather_kernel(
    n, zn, reach, gene_ref, idx_ref, lw_ref, table, idx, lw, zs, zr, ns, nr, rs, rr, ls, lr
):
    i = lax.axis_index("snp")
    q = lax.axis_index("prog")
    odd = i % 2
    step = 2 * odd - 1
    rows, cols = gene_ref.shape
    snps = idx_ref.shape[1]
    mate = i - step
    near = i + step
    far = i - 2 * step
    has_near = (near >= 0) & (near < n)
    has_far = (far >= 0) & (far < n)
    mate_near = mate - step
    mate_has_near = (mate_near >= 0) & (mate_near < n)

    barrier = pltpu.get_barrier_semaphore()

    def greet(target):
        pl.semaphore_signal(barrier, inc=1, device_id=target, device_id_type=MESH)

    for o in range(1, zn):
        greet((i, (q + o) % zn))
    greet((mate, q))

    @pl.when(has_near)
    def _():
        greet((near, q))

    @pl.when(has_far)
    def _():
        greet((far, q))

    far_from = i + 2 * step
    has_far_from = (far_from >= 0) & (far_from < n)

    @pl.when(has_far_from)
    def _():
        greet((far_from, q))

    own_rows = pl.ds(pl.multiple_of(q * cols, cols), cols)
    table[own_rows, 2 * rows : 3 * rows] = gene_ref[...].T
    idx[:, reach : reach + snps] = idx_ref[...]
    lw[:, reach : reach + snps] = lw_ref[...]

    def zero(slot):
        table[:, slot * rows : (slot + 1) * rows] = jnp.zeros((table.shape[0], rows), BF16)

    @pl.when(i < 2)
    def _():
        zero(0)

    @pl.when(i < 1)
    def _():
        zero(1)
        idx[:, :reach] = jnp.zeros((idx.shape[0], reach), jnp.int32)
        lw[:, :reach] = jnp.zeros((lw.shape[0], reach), F32)

    @pl.when(i > n - 2)
    def _():
        zero(3)
        idx[:, reach + snps :] = jnp.zeros((idx.shape[0], reach), jnp.int32)
        lw[:, reach + snps :] = jnp.zeros((lw.shape[0], reach), F32)

    @pl.when(i > n - 3)
    def _():
        zero(4)

    peers = zn
    for there in (has_near, has_far, has_far_from):
        peers = peers + there.astype(jnp.int32)
    pl.semaphore_wait(barrier, peers)

    def piece(slot, z):
        return table.at[
            pl.ds(pl.multiple_of(z * cols, cols), cols),
            pl.ds(pl.multiple_of(slot * rows, rows), rows),
        ]

    def z_copy(o):
        return pltpu.make_async_remote_copy(
            src_ref=piece(2, q),
            dst_ref=piece(2, q),
            send_sem=zs.at[o - 1],
            recv_sem=zr.at[o - 1],
            device_id=(i, (q + o) % zn),
            device_id_type=MESH,
        )

    def own_copy(kind, o):
        z = (q - o + zn) % zn
        target = (mate, near, far)[kind]
        return pltpu.make_async_remote_copy(
            src_ref=piece(2, z),
            dst_ref=piece(i - target + 2, z),
            send_sem=ns.at[kind, o],
            recv_sem=nr.at[kind, o],
            device_id=(target, q),
            device_id_type=MESH,
        )

    def own_arrive(kind, o):
        z = (q - o + zn) % zn
        source = (mate, near, far_from)[kind]
        return pltpu.make_async_remote_copy(
            src_ref=piece(2, z),
            dst_ref=piece(source - i + 2, z),
            send_sem=ns.at[kind, o],
            recv_sem=nr.at[kind, o],
            device_id=(mate, q),
            device_id_type=MESH,
        )

    def relay(o):
        z = (q - o + zn) % zn
        return pltpu.make_async_remote_copy(
            src_ref=piece(near - i + 2, z),
            dst_ref=piece(near - mate + 2, z),
            send_sem=rs.at[o],
            recv_sem=rr.at[o],
            device_id=(mate, q),
            device_id_type=MESH,
        )

    def relay_arrive(o):
        z = (q - o + zn) % zn
        return pltpu.make_async_remote_copy(
            src_ref=piece(2, z),
            dst_ref=piece(mate_near - i + 2, z),
            send_sem=rs.at[o],
            recv_sem=rr.at[o],
            device_id=(mate, q),
            device_id_type=MESH,
        )

    def link_copy(which, up):
        ref = (idx, lw)[which]
        src = pl.ds(snps if up else reach, reach)
        dst = pl.ds(0 if up else reach + snps, reach)
        return pltpu.make_async_remote_copy(
            src_ref=ref.at[:, src],
            dst_ref=ref.at[:, dst],
            send_sem=ls.at[which, up],
            recv_sem=lr.at[which, up],
            device_id=(i + 1 if up else i - 1, q),
            device_id_type=MESH,
        )

    for o in range(1, zn):
        z_copy(o).start()

    def send_own(o):
        own_copy(0, o).start()

        @pl.when(has_near)
        def _():
            own_copy(1, o).start()

        @pl.when(has_far)
        def _():
            own_copy(2, o).start()

    send_own(0)

    @pl.when(i < n - 1)
    def _():
        link_copy(0, 1).start()
        link_copy(1, 1).start()

    @pl.when(i > 0)
    def _():
        link_copy(0, 0).start()
        link_copy(1, 0).start()

    for o in range(1, zn):
        pltpu.make_async_remote_copy(
            src_ref=piece(2, q),
            dst_ref=piece(2, (q - o + zn) % zn),
            send_sem=zs.at[o - 1],
            recv_sem=zr.at[o - 1],
            device_id=(mate, q),
            device_id_type=MESH,
        ).wait_recv()
        send_own(o)

    @pl.when(has_near)
    def _():
        for o in range(zn):
            own_arrive(1, o).wait_recv()
            relay(o).start()

    for o in range(zn):
        own_arrive(0, o).wait_recv()

    @pl.when(has_far_from)
    def _():
        for o in range(zn):
            own_arrive(2, o).wait_recv()

    @pl.when(mate_has_near)
    def _():
        for o in range(zn):
            relay_arrive(o).wait_recv()

    @pl.when(i < n - 1)
    def _():
        for which in range(2):
            link_copy(which, 0).wait_recv()
            link_copy(which, 1).wait_send()

    @pl.when(i > 0)
    def _():
        for which in range(2):
            link_copy(which, 1).wait_recv()
            link_copy(which, 0).wait_send()

    for o in range(1, zn):
        z_copy(o).wait_send()
    for o in range(zn):
        own_copy(0, o).wait_send()

    @pl.when(has_near)
    def _():
        for o in range(zn):
            own_copy(1, o).wait_send()
            relay(o).wait_send()

    @pl.when(has_far)
    def _():
        for o in range(zn):
            own_copy(2, o).wait_send()


def score_kernel(
    band, jk_ref, scale_ref, table, idx, lw, levels, sw, out, sq, ann, square
):
    unit = pl.program_id(0)
    tile = levels.shape[2]
    rows = table.shape[1] // 5
    group = levels.shape[0]
    wide = group * tile
    chunks = ann.shape[1] // wide
    reach = band // 2 * tile
    span = 3 * rows

    def annotate(start, slot):
        at = pl.ds(pl.multiple_of(start, wide), wide)
        first = (lax.axis_index("snp") - 2 + slot) * rows
        local = idx[:, at] - first
        strength = lw[:, at]
        gene = lax.broadcasted_iota(jnp.int32, (span, wide), 0)
        mix = jnp.zeros((span, wide), F32)
        for link in range(idx.shape[0]):
            mix = jnp.where(
                local[link : link + 1] == gene, strength[link : link + 1], mix
            )
        ann[:, at] = jnp.dot(
            table[:, slot * rows : slot * rows + span],
            mix.astype(BF16),
            preferred_element_type=F32,
        ).astype(BF16)

    @pl.when(unit == 0)
    def _():
        square[...] = jnp.zeros_like(square)
        for start in range(0, reach, wide):
            annotate(start, 0)
            annotate(ann.shape[1] - reach + start, 2)

        @pl.loop(reach // wide, chunks - reach // wide)
        def _(c):
            annotate(c * wide, 1)

    blocks = []
    for g in range(group):
        parts = [jnp.zeros((tile, tile), BF16)] * g
        for d in range(band):
            s = scale_ref[unit * group + g, d]
            parts.append((levels[g, d].astype(F32) * s).astype(BF16))
        parts += [jnp.zeros((tile, tile), BF16)] * (group - 1 - g)
        blocks.append(jnp.concatenate(parts, axis=1))
    mixer = jnp.concatenate(blocks, axis=0)
    window = ann[:, pl.ds(pl.multiple_of(unit * wide, wide), mixer.shape[1])]
    score = nt_dot(window, mixer).astype(BF16).astype(F32)
    weighted = sw[...] * score
    out[...] = weighted.astype(BF16)
    part = weighted * score
    part = sum(part[:, a : a + 128] for a in range(0, wide, 128))
    j = jk_ref[0, unit]
    square[j] += part

    @pl.when(unit == pl.num_programs(0) - 1)
    def _():
        ones = jnp.ones((8, 128), F32)
        for j in range(JK_DEV):
            line = nt_dot(ones, square[j], precision=lax.Precision.HIGHEST)
            for r in range(sq.shape[1]):
                sq[j, r : r + 1, :] = line[0:1, r * 128 : (r + 1) * 128]


def cross_kernel(
    n, w_ref, z_ref, mask_ref, sq_ref, crossed, total, sq_total,
    acc, c_out, c_in, p_out, p_in, q_out, q_in,
    cs, cr, ps, pr, gs, gr, hs, hr, qs, qr,
):
    i = lax.axis_index("snp")
    z = lax.axis_index("prog")
    c = i % 2
    m = i // 2
    chips = n // 2
    mate = i + 1 - 2 * c
    chunks = ROW_CHUNKS
    rows = w_ref.shape[0] // chunks
    half = rows // 2
    own = half // chips
    half_s = w_ref.shape[1] // 2

    barrier = pltpu.get_barrier_semaphore()
    for o in range(1, n):
        pl.semaphore_signal(barrier, inc=1, device_id=((i + o) % n, z), device_id_type=MESH)
    q_out[...] = sq_ref[0] + sq_ref[1] + sq_ref[2]

    def remote(src, dst, s, r, device):
        return pltpu.make_async_remote_copy(
            src_ref=src, dst_ref=dst, send_sem=s, recv_sem=r,
            device_id=(device, z), device_id_type=MESH,
        )

    def sq_copy(o):
        return remote(q_out, q_in.at[o - 1], qs.at[o - 1], qr.at[o - 1], (i + o) % n)

    def core_copy(k):
        return remote(c_out.at[k], c_in.at[k], cs.at[k], cr.at[k], mate)

    def peer_copy(k, o):
        owner = (m + o) % chips
        return remote(
            p_out.at[k, pl.ds(pl.multiple_of(owner * own, own), own)],
            p_in.at[k, o - 1], ps.at[k, o - 1], pr.at[k, o - 1], owner * 2 + c,
        )

    def place(k, core, chip):
        return pl.ds(pl.multiple_of(k * rows + core * half + chip * own, own), own)

    def gather_copy(k, o):
        at = total.at[place(k, c, m)]
        return remote(at, at, gs.at[k, o - 1], gr.at[k, o - 1], (m + o) % chips * 2 + c)

    def gather_arrive(k, o):
        at = total.at[place(k, c, (m + chips - o) % chips)]
        return remote(at, at, gs.at[k, o - 1], gr.at[k, o - 1], mate)

    def half_copy(k, core):
        at = total.at[pl.ds(pl.multiple_of(k * rows + core * half, half), half)]
        return remote(at, at, hs.at[k], hr.at[k], mate)

    def compute(k):
        at = slice(k * rows, (k + 1) * rows)
        acc[at, :] = jnp.dot(w_ref[at, :], z_ref[...], preferred_element_type=F32)
        away = pl.ds(pl.multiple_of(k * rows + (1 - c) * half, half), half)
        c_out[k] = acc[away, :].astype(BF16)

    def after_core(k):
        core_copy(k).wait_recv()
        home = pl.ds(pl.multiple_of(k * rows + c * half, half), half)
        p_out[k] = (acc[home, :] + c_in[k].astype(F32)).astype(BF16)
        for o in range(1, chips):
            peer_copy(k, o).start()

    def after_peers(k):
        for o in range(1, chips):
            peer_copy(k, o).wait_recv()
        s = p_out[k, pl.ds(pl.multiple_of(m * own, own), own)].astype(F32)
        for o in range(1, chips):
            s = s + p_in[k, o - 1].astype(F32)
        total[place(k, c, m), :] = s.astype(BF16)
        for o in range(1, chips):
            gather_copy(k, o).start()

    def after_gather(k):
        for o in range(1, chips):
            gather_arrive(k, o).wait_recv()
        half_copy(k, c).start()

    def split(k):
        at = slice(k * rows, (k + 1) * rows)
        first = jnp.dot(
            w_ref[at, :half_s] * mask_ref[0:1, :half_s], z_ref[:half_s, :],
            preferred_element_type=F32,
        )
        last = jnp.dot(
            w_ref[at, half_s:] * mask_ref[1:2, half_s:], z_ref[half_s:, :],
            preferred_element_type=F32,
        )
        crossed[0, at, :] = first.astype(BF16)
        crossed[2, at, :] = last.astype(BF16)
        crossed[1, at, :] = (acc[at, :] - first - last).astype(BF16)

    compute(0)
    pl.semaphore_wait(barrier, n - 1)
    core_copy(0).start()
    for o in range(1, n):
        sq_copy(o).start()
    for k in range(1, chunks):
        compute(k)
        core_copy(k).start()
        after_core(k - 1)
    split(0)
    after_core(chunks - 1)
    after_peers(0)
    for k in range(1, chunks):
        split(k)
        after_peers(k)
        after_gather(k - 1)
    after_gather(chunks - 1)
    s = q_out[...]
    for o in range(1, n):
        sq_copy(o).wait_recv()
        s = s + q_in[o - 1]
    sq_total[...] = s
    for o in range(1, n):
        sq_copy(o).wait_send()
    for k in range(chunks):
        half_copy(k, 1 - c).wait_recv()
        half_copy(k, c).wait_send()
        core_copy(k).wait_send()
        for o in range(1, chips):
            peer_copy(k, o).wait_send()
            gather_copy(k, o).wait_send()


def estimate_kernel(crossed, total, leave, keep, delete_one, own):
    whole = total[...].astype(F32)
    for j in range(JK_DEV):
        part = crossed[j].astype(F32)
        delete_one[j] = ((whole - part) * leave[j]).astype(BF16)
        own[j] = (part * keep[j]).astype(BF16)


def on_device(
    n, zn, gene_score, link_gene, link_weight, ld_levels, ld_scale, snp_weight, trait_z, jk_unit
):
    unit_count = jk_unit.shape[1]
    snps, links = link_gene.shape
    tiles, band, tile, _ = ld_levels.shape
    reach = band // 2 * tile
    rows, cols = gene_score.shape
    programs = cols * zn
    traits = trait_z.shape[1]
    wide = snps // unit_count
    group = wide // tile
    vmem = pl.BlockSpec(memory_space=pltpu.VMEM)
    smem = pl.BlockSpec(memory_space=pltpu.SMEM)
    dma = pltpu.SemaphoreType.DMA
    limit = 60 * 1024 * 1024

    table, idx, lw = pl.pallas_call(
        functools.partial(gather_kernel, n, zn, reach),
        out_shape=(
            jax.ShapeDtypeStruct((programs, 5 * rows), BF16),
            jax.ShapeDtypeStruct((links, snps + 2 * reach), jnp.int32),
            jax.ShapeDtypeStruct((links, snps + 2 * reach), F32),
        ),
        in_specs=[vmem] * 3,
        out_specs=(vmem,) * 3,
        scratch_shapes=[
            dma((zn - 1,)), dma((zn - 1,)), dma((3, zn)), dma((3, zn)),
            dma((zn,)), dma((zn,)), dma((2, 2)), dma((2, 2)),
        ],
        compiler_params=pltpu.CompilerParams(collective_id=0, has_side_effects=True),
        name="gather_genes",
    )(gene_score, link_gene.T, link_weight.T.astype(F32))

    weighted, square = pl.pallas_call(
        functools.partial(score_kernel, band),
        grid=(unit_count,),
        out_shape=(
            jax.ShapeDtypeStruct((programs, snps), BF16),
            jax.ShapeDtypeStruct((JK_DEV, programs // 128, 128), F32),
        ),
        in_specs=[
            smem,
            smem,
            vmem,
            vmem,
            vmem,
            pl.BlockSpec((group, band, tile, tile), lambda u: (u, 0, 0, 0)),
            pl.BlockSpec((1, wide), lambda u: (0, u)),
        ],
        out_specs=(
            pl.BlockSpec((programs, wide), lambda u: (0, u)),
            pl.BlockSpec((JK_DEV, programs // 128, 128), lambda u: (0, 0, 0)),
        ),
        scratch_shapes=[
            pltpu.VMEM((programs, snps + 2 * reach), BF16),
            pltpu.VMEM((JK_DEV, programs, 128), F32),
        ],
        compiler_params=pltpu.CompilerParams(vmem_limit_bytes=limit),
        name="ld_scores",
    )(jk_unit, ld_scale, table, idx, lw, ld_levels, snp_weight[None])

    ends = jnp.array([0, JK_DEV - 1], jnp.int32)
    mask = jnp.repeat(jk_unit[0][None] == ends[:, None], wide, axis=1).astype(BF16)
    mask = jnp.pad(mask, ((0, 14), (0, 0)))

    k = ROW_CHUNKS
    half = programs // k // 2
    chips = n // 2
    crossed, total, sq_total = pl.pallas_call(
        functools.partial(cross_kernel, n),
        out_shape=(
            jax.ShapeDtypeStruct((JK_DEV, programs, traits), BF16),
            jax.ShapeDtypeStruct((programs, traits), BF16),
            jax.ShapeDtypeStruct((programs // 128, 128), F32),
        ),
        in_specs=[vmem] * 4,
        out_specs=(vmem,) * 3,
        scratch_shapes=[
            pltpu.VMEM((programs, traits), F32),
            pltpu.VMEM((k, half, traits), BF16),
            pltpu.VMEM((k, half, traits), BF16),
            pltpu.VMEM((k, half, traits), BF16),
            pltpu.VMEM((k, chips - 1, half // chips, traits), BF16),
            pltpu.VMEM((programs // 128, 128), F32),
            pltpu.VMEM((n - 1, programs // 128, 128), F32),
            dma((k,)), dma((k,)),
            dma((k, chips - 1)), dma((k, chips - 1)),
            dma((k, chips - 1)), dma((k, chips - 1)),
            dma((k,)), dma((k,)),
            dma((n - 1,)), dma((n - 1,)),
        ],
        compiler_params=pltpu.CompilerParams(
            collective_id=1, has_side_effects=True, vmem_limit_bytes=limit
        ),
        name="cross_total",
    )(weighted, trait_z, mask, square)

    keep = (1.0 / jnp.sqrt(square)).reshape(JK_DEV, programs, 1)
    leave = (1.0 / jnp.sqrt(sq_total[None] - square)).reshape(JK_DEV, programs, 1)
    block = programs // 8
    whole = pl.BlockSpec((JK_DEV, block, traits), lambda p: (0, p, 0))
    column = pl.BlockSpec((JK_DEV, block, 1), lambda p: (0, p, 0))
    return pl.pallas_call(
        estimate_kernel,
        grid=(programs // block,),
        out_shape=(jax.ShapeDtypeStruct((JK_DEV, programs, traits), BF16),) * 2,
        in_specs=[whole, pl.BlockSpec((block, traits), lambda p: (p, 0)), column, column],
        out_specs=(whole, whole),
        compiler_params=pltpu.CompilerParams(vmem_limit_bytes=limit),
        name="estimates",
    )(crossed, total, leave, keep)


def solution(mesh):
    placed = (
        P("snp", "prog"),
        P("snp", None),
        P("snp", None),
        P("snp", None, None, None),
        P("snp", None),
        P("snp"),
        P("snp", "prog"),
        P("snp", None),
    )
    return jax.shard_map(
        functools.partial(on_device, mesh.shape["snp"], mesh.shape["prog"]),
        mesh=mesh,
        in_specs=placed,
        out_specs=(P("snp", None, "prog"), P("snp", None, "prog")),
        check_vma=False,
    )
```

```python
import functools

import jax
import jax.numpy as jnp
from jax import lax
from jax.experimental import pallas as pl
from jax.experimental.pallas import tpu as pltpu
from jax.sharding import PartitionSpec as P

JK_DEV = 3
MESH = pl.DeviceIdType.MESH
F32 = jnp.float32
BF16 = jnp.bfloat16
ROW_CHUNKS = 4


def nt_dot(a, b, **kw):
    return lax.dot_general(a, b, (((1,), (1,)), ((), ())), preferred_element_type=F32, **kw)


def one_hot(local, strength, span):
    gene = lax.broadcasted_iota(jnp.int32, (span, local.shape[1]), 0)
    mix = jnp.zeros(gene.shape, F32)
    for link in range(local.shape[0]):
        mix = jnp.where(local[link : link + 1] == gene, strength[link : link + 1], mix)
    return mix.astype(BF16)


def gather_kernel(
    n, zn, reach, wide, gene_ref, idx_ref, lw_ref, table, idx, lw, mix, zs, zr, ns, nr, rs, rr, ls, lr
):
    i = lax.axis_index("snp")
    q = lax.axis_index("prog")
    odd = i % 2
    step = 2 * odd - 1
    rows, cols = gene_ref.shape
    snps = idx_ref.shape[1]
    mate = i - step
    near = i + step
    far = i - 2 * step
    has_near = (near >= 0) & (near < n)
    has_far = (far >= 0) & (far < n)
    mate_near = mate - step
    mate_has_near = (mate_near >= 0) & (mate_near < n)

    barrier = pltpu.get_barrier_semaphore()

    def greet(target):
        pl.semaphore_signal(barrier, inc=1, device_id=target, device_id_type=MESH)

    for o in range(1, zn):
        greet((i, (q + o) % zn))
    greet((mate, q))

    @pl.when(has_near)
    def _():
        greet((near, q))

    @pl.when(has_far)
    def _():
        greet((far, q))

    far_from = i + 2 * step
    has_far_from = (far_from >= 0) & (far_from < n)

    @pl.when(has_far_from)
    def _():
        greet((far_from, q))

    own_rows = pl.ds(pl.multiple_of(q * cols, cols), cols)
    table[own_rows, 2 * rows : 3 * rows] = gene_ref[...].T
    idx[:, reach : reach + snps] = idx_ref[...]
    lw[:, reach : reach + snps] = lw_ref[...].astype(F32)

    def zero(slot):
        table[:, slot * rows : (slot + 1) * rows] = jnp.zeros((table.shape[0], rows), BF16)

    @pl.when(i < 2)
    def _():
        zero(0)

    @pl.when(i < 1)
    def _():
        zero(1)
        idx[:, :reach] = jnp.zeros((idx.shape[0], reach), jnp.int32)
        lw[:, :reach] = jnp.zeros((lw.shape[0], reach), F32)

    @pl.when(i > n - 2)
    def _():
        zero(3)
        idx[:, reach + snps :] = jnp.zeros((idx.shape[0], reach), jnp.int32)
        lw[:, reach + snps :] = jnp.zeros((lw.shape[0], reach), F32)

    @pl.when(i > n - 3)
    def _():
        zero(4)

    peers = zn
    for there in (has_near, has_far, has_far_from):
        peers = peers + there.astype(jnp.int32)
    pl.semaphore_wait(barrier, peers)

    def piece(slot, z):
        return table.at[
            pl.ds(pl.multiple_of(z * cols, cols), cols),
            pl.ds(pl.multiple_of(slot * rows, rows), rows),
        ]

    def z_copy(o):
        return pltpu.make_async_remote_copy(
            src_ref=piece(2, q),
            dst_ref=piece(2, q),
            send_sem=zs.at[o - 1],
            recv_sem=zr.at[o - 1],
            device_id=(i, (q + o) % zn),
            device_id_type=MESH,
        )

    def own_copy(kind, o):
        z = (q - o + zn) % zn
        target = (mate, near, far)[kind]
        return pltpu.make_async_remote_copy(
            src_ref=piece(2, z),
            dst_ref=piece(i - target + 2, z),
            send_sem=ns.at[kind, o],
            recv_sem=nr.at[kind, o],
            device_id=(target, q),
            device_id_type=MESH,
        )

    def own_arrive(kind, o):
        z = (q - o + zn) % zn
        source = (mate, near, far_from)[kind]
        return pltpu.make_async_remote_copy(
            src_ref=piece(2, z),
            dst_ref=piece(source - i + 2, z),
            send_sem=ns.at[kind, o],
            recv_sem=nr.at[kind, o],
            device_id=(mate, q),
            device_id_type=MESH,
        )

    def relay(o):
        z = (q - o + zn) % zn
        return pltpu.make_async_remote_copy(
            src_ref=piece(near - i + 2, z),
            dst_ref=piece(near - mate + 2, z),
            send_sem=rs.at[o],
            recv_sem=rr.at[o],
            device_id=(mate, q),
            device_id_type=MESH,
        )

    def relay_arrive(o):
        z = (q - o + zn) % zn
        return pltpu.make_async_remote_copy(
            src_ref=piece(2, z),
            dst_ref=piece(mate_near - i + 2, z),
            send_sem=rs.at[o],
            recv_sem=rr.at[o],
            device_id=(mate, q),
            device_id_type=MESH,
        )

    def link_copy(which, up):
        ref = (idx, lw)[which]
        src = pl.ds(snps if up else reach, reach)
        dst = pl.ds(0 if up else reach + snps, reach)
        return pltpu.make_async_remote_copy(
            src_ref=ref.at[:, src],
            dst_ref=ref.at[:, dst],
            send_sem=ls.at[which, up],
            recv_sem=lr.at[which, up],
            device_id=(i + 1 if up else i - 1, q),
            device_id_type=MESH,
        )

    chunks = snps // wide

    def build(lo, hi):
        @pl.loop(lo, hi)
        def _(c):
            at = pl.ds(pl.multiple_of(c * wide, wide), wide)
            inner = pl.ds(pl.multiple_of(c * wide + reach, wide), wide)
            mix[:, at] = one_hot(idx[:, inner] - (i - 1) * rows, lw[:, inner], 3 * rows)

    for o in range(1, zn):
        z_copy(o).start()

    def send_own(o):
        own_copy(0, o).start()

        @pl.when(has_near)
        def _():
            own_copy(1, o).start()

        @pl.when(has_far)
        def _():
            own_copy(2, o).start()

    send_own(0)

    @pl.when(i < n - 1)
    def _():
        link_copy(0, 1).start()
        link_copy(1, 1).start()

    @pl.when(i > 0)
    def _():
        link_copy(0, 0).start()
        link_copy(1, 0).start()

    for o in range(1, zn):
        build((o - 1) * chunks // zn, o * chunks // zn)
        pltpu.make_async_remote_copy(
            src_ref=piece(2, q),
            dst_ref=piece(2, (q - o + zn) % zn),
            send_sem=zs.at[o - 1],
            recv_sem=zr.at[o - 1],
            device_id=(mate, q),
            device_id_type=MESH,
        ).wait_recv()
        send_own(o)

    build((zn - 1) * chunks // zn, chunks)

    @pl.when(has_near)
    def _():
        for o in range(zn):
            own_arrive(1, o).wait_recv()
            relay(o).start()

    for o in range(zn):
        own_arrive(0, o).wait_recv()

    @pl.when(has_far_from)
    def _():
        for o in range(zn):
            own_arrive(2, o).wait_recv()

    @pl.when(mate_has_near)
    def _():
        for o in range(zn):
            relay_arrive(o).wait_recv()

    @pl.when(i < n - 1)
    def _():
        for which in range(2):
            link_copy(which, 0).wait_recv()
            link_copy(which, 1).wait_send()

    @pl.when(i > 0)
    def _():
        for which in range(2):
            link_copy(which, 1).wait_recv()
            link_copy(which, 0).wait_send()

    for o in range(1, zn):
        z_copy(o).wait_send()
    for o in range(zn):
        own_copy(0, o).wait_send()

    @pl.when(has_near)
    def _():
        for o in range(zn):
            own_copy(1, o).wait_send()
            relay(o).wait_send()

    @pl.when(has_far)
    def _():
        for o in range(zn):
            own_copy(2, o).wait_send()


def score_kernel(
    band, jk_ref, scale_ref, table, idx, lw, mix, levels, sw, out, sq, mask, ann, square
):
    unit = pl.program_id(0)
    tile = levels.shape[2]
    rows = table.shape[1] // 5
    group = levels.shape[0]
    wide = group * tile
    reach = band // 2 * tile
    span = 3 * rows

    def annotate(start, slot):
        at = pl.ds(pl.multiple_of(start, wide), wide)
        first = (lax.axis_index("snp") - 2 + slot) * rows
        ann[:, at] = jnp.dot(
            table[:, slot * rows : slot * rows + span],
            one_hot(idx[:, at] - first, lw[:, at], span),
            preferred_element_type=F32,
        ).astype(BF16)

    @pl.when(unit == 0)
    def _():
        square[...] = jnp.zeros_like(square)
        for start in range(0, reach, wide):
            annotate(start, 0)
            annotate(ann.shape[1] - reach + start, 2)

        @pl.loop(0, mix.shape[1] // wide)
        def _(c):
            ann[:, pl.ds(pl.multiple_of(c * wide + reach, wide), wide)] = jnp.dot(
                table[:, rows : 4 * rows],
                mix[:, pl.ds(pl.multiple_of(c * wide, wide), wide)],
                preferred_element_type=F32,
            ).astype(BF16)

    blocks = []
    for g in range(group):
        parts = [jnp.zeros((tile, tile), BF16)] * g
        for d in range(band):
            s = scale_ref[unit * group + g, d]
            parts.append((levels[g, d].astype(F32) * s).astype(BF16))
        parts += [jnp.zeros((tile, tile), BF16)] * (group - 1 - g)
        blocks.append(jnp.concatenate(parts, axis=1))
    mixer = jnp.concatenate(blocks, axis=0)
    window = ann[:, pl.ds(pl.multiple_of(unit * wide, wide), mixer.shape[1])]
    score = nt_dot(window, mixer).astype(BF16).astype(F32)
    weighted = sw[...] * score
    out[...] = weighted.astype(BF16)
    part = weighted * score
    part = sum(part[:, a : a + 128] for a in range(0, wide, 128))
    j = jk_ref[0, unit]
    square[j] += part
    line = lax.broadcasted_iota(jnp.int32, mask.shape, 0)
    mine = (line == 0) & (j == 0) | (line == 1) & (j == JK_DEV - 1)
    mask[...] = jnp.where(mine, 1.0, 0.0).astype(BF16)

    @pl.when(unit == pl.num_programs(0) - 1)
    def _():
        ones = jnp.ones((8, 128), F32)
        for j in range(JK_DEV):
            line = nt_dot(ones, square[j], precision=lax.Precision.HIGHEST)
            for r in range(sq.shape[1]):
                sq[j, r : r + 1, :] = line[0:1, r * 128 : (r + 1) * 128]


def cross_kernel(
    n, w_ref, z_ref, mask_ref, sq_ref, crossed, total, sq_total,
    acc, c_out, c_in, p_out, p_in, q_out, q_in,
    cs, cr, ps, pr, gs, gr, hs, hr, qs, qr,
):
    i = lax.axis_index("snp")
    z = lax.axis_index("prog")
    c = i % 2
    m = i // 2
    chips = n // 2
    mate = i + 1 - 2 * c
    chunks = ROW_CHUNKS
    rows = w_ref.shape[0] // chunks
    half = rows // 2
    stages = chips.bit_length() - 1
    half_s = w_ref.shape[1] // 2

    barrier = pltpu.get_barrier_semaphore()
    for o in range(1, n):
        pl.semaphore_signal(barrier, inc=1, device_id=((i + o) % n, z), device_id_type=MESH)
    q_out[...] = sq_ref[0] + sq_ref[1] + sq_ref[2]

    def remote(src, dst, s, r, device):
        return pltpu.make_async_remote_copy(
            src_ref=src, dst_ref=dst, send_sem=s, recv_sem=r,
            device_id=(device, z), device_id_type=MESH,
        )

    def sq_copy(o):
        return remote(q_out, q_in.at[o - 1], qs.at[o - 1], qr.at[o - 1], (i + o) % n)

    def core_copy(k):
        return remote(c_out.at[k], c_in.at[k], cs.at[k], cr.at[k], mate)

    sides, mates, offsets = [], [], [0]
    for t in range(stages):
        low, high = 2**t, 2 ** (stages - 1 - t)
        side = (1 - c) * (m // low % 2) + c * (m // high % 2)
        weight = (1 - c) * low + c * high
        sides.append(side)
        mates.append((m + weight * (1 - 2 * side)) * 2 + c)
        offsets.append(offsets[t] + side * (half >> (t + 1)))

    def part(base, size):
        return pl.ds(pl.multiple_of(base, size), size)

    def peer_copy(k, t):
        size = half >> (t + 1)
        return remote(
            p_out.at[k, part(offsets[t] + (1 - sides[t]) * size, size)],
            p_in.at[k, pl.ds(half - 2 * size, size)], ps.at[k, t], pr.at[k, t], mates[t],
        )

    def gather_copy(k, t):
        size = half >> (t + 1)
        at = total.at[part(k * rows + c * half + offsets[t + 1], size)]
        return remote(at, at, gs.at[k, t], gr.at[k, t], mates[t])

    def gather_arrive(k, t):
        size = half >> (t + 1)
        at = total.at[part(k * rows + c * half + offsets[t] + (1 - sides[t]) * size, size)]
        return remote(at, at, gs.at[k, t], gr.at[k, t], mates[t])

    def half_copy(k, core):
        at = total.at[pl.ds(pl.multiple_of(k * rows + core * half, half), half)]
        return remote(at, at, hs.at[k], hr.at[k], mate)

    def compute(k):
        at = slice(k * rows, (k + 1) * rows)
        acc[at, :] = jnp.dot(w_ref[at, :], z_ref[...], preferred_element_type=F32)
        away = pl.ds(pl.multiple_of(k * rows + (1 - c) * half, half), half)
        c_out[k] = acc[away, :].astype(BF16)

    def after_core(k):
        core_copy(k).wait_recv()
        home = pl.ds(pl.multiple_of(k * rows + c * half, half), half)
        p_out[k] = (acc[home, :] + c_in[k].astype(F32)).astype(BF16)
        peer_copy(k, 0).start()

    def after_peer(k, t):
        size = half >> (t + 1)
        peer_copy(k, t).wait_recv()
        at = part(offsets[t + 1], size)
        s = p_out[k, at].astype(F32) + p_in[k, half - 2 * size : half - size].astype(F32)
        if t + 1 < stages:
            p_out[k, at] = s.astype(BF16)
            peer_copy(k, t + 1).start()
        else:
            total[part(k * rows + c * half + offsets[t + 1], size), :] = s.astype(BF16)
            gather_copy(k, t).start()

    def after_gather(k, t):
        gather_arrive(k, t).wait_recv()
        if t:
            gather_copy(k, t - 1).start()
        else:
            half_copy(k, c).start()

    def split(k):
        at = slice(k * rows, (k + 1) * rows)
        first = jnp.dot(
            w_ref[at, :half_s] * mask_ref[0:1, :half_s], z_ref[:half_s, :],
            preferred_element_type=F32,
        )
        last = jnp.dot(
            w_ref[at, half_s:] * mask_ref[1:2, half_s:], z_ref[half_s:, :],
            preferred_element_type=F32,
        )
        crossed[0, at, :] = first.astype(BF16)
        crossed[2, at, :] = last.astype(BF16)
        crossed[1, at, :] = (acc[at, :] - first - last).astype(BF16)

    compute(0)
    pl.semaphore_wait(barrier, n - 1)
    core_copy(0).start()
    for o in range(1, n):
        sq_copy(o).start()
    steps = [after_core]
    steps += [functools.partial(after_peer, t=t) for t in range(stages)]
    steps += [functools.partial(after_gather, t=t) for t in reversed(range(stages))]
    for slot in range(max(2 * chunks - 1, chunks + len(steps) - 1)):
        if slot < chunks - 1:
            compute(slot + 1)
            core_copy(slot + 1).start()
        elif slot < 2 * chunks - 1:
            split(slot + 1 - chunks)
        for k in range(chunks):
            if 0 <= slot - k < len(steps):
                steps[slot - k](k)
    s = q_out[...]
    for o in range(1, n):
        sq_copy(o).wait_recv()
        s = s + q_in[o - 1]
    sq_total[...] = s
    for o in range(1, n):
        sq_copy(o).wait_send()
    for k in range(chunks):
        half_copy(k, 1 - c).wait_recv()
        half_copy(k, c).wait_send()
        core_copy(k).wait_send()
        for t in range(stages):
            peer_copy(k, t).wait_send()
            gather_copy(k, t).wait_send()


def estimate_kernel(crossed, total, sq, sq_total, delete_one, own):
    block, traits = total.shape
    line = pl.ds(pl.program_id(0), 1)
    whole = total[...].astype(F32)

    def column(row):
        turned = jnp.broadcast_to(1.0 / jnp.sqrt(row), (block, block)).T
        return jnp.concatenate([turned] * (traits // block), axis=1)

    for j in range(JK_DEV):
        part = crossed[j].astype(F32)
        row = sq[j, line, :]
        leave = column(sq_total[line, :] - row)
        delete_one[j] = ((whole - part) * leave).astype(BF16)
        own[j] = (part * column(row)).astype(BF16)


def on_device(
    n, zn, gene_score, link_gene, link_weight, ld_levels, ld_scale, snp_weight, trait_z, jk_unit
):
    unit_count = jk_unit.shape[1]
    snps, links = link_gene.shape
    tiles, band, tile, _ = ld_levels.shape
    reach = band // 2 * tile
    rows, cols = gene_score.shape
    programs = cols * zn
    traits = trait_z.shape[1]
    wide = snps // unit_count
    group = wide // tile
    vmem = pl.BlockSpec(memory_space=pltpu.VMEM)
    smem = pl.BlockSpec(memory_space=pltpu.SMEM)
    dma = pltpu.SemaphoreType.DMA
    limit = 60 * 1024 * 1024

    table, idx, lw, mix = pl.pallas_call(
        functools.partial(gather_kernel, n, zn, reach, wide),
        out_shape=(
            jax.ShapeDtypeStruct((programs, 5 * rows), BF16),
            jax.ShapeDtypeStruct((links, snps + 2 * reach), jnp.int32),
            jax.ShapeDtypeStruct((links, snps + 2 * reach), F32),
            jax.ShapeDtypeStruct((3 * rows, snps), BF16),
        ),
        in_specs=[vmem] * 3,
        out_specs=(vmem,) * 4,
        scratch_shapes=[
            dma((zn - 1,)), dma((zn - 1,)), dma((3, zn)), dma((3, zn)),
            dma((zn,)), dma((zn,)), dma((2, 2)), dma((2, 2)),
        ],
        compiler_params=pltpu.CompilerParams(collective_id=0, has_side_effects=True),
        name="gather_genes",
    )(gene_score, link_gene.T, link_weight.T)

    weighted, square, mask = pl.pallas_call(
        functools.partial(score_kernel, band),
        grid=(unit_count,),
        out_shape=(
            jax.ShapeDtypeStruct((programs, snps), BF16),
            jax.ShapeDtypeStruct((JK_DEV, programs // 128, 128), F32),
            jax.ShapeDtypeStruct((16, snps), BF16),
        ),
        in_specs=[
            smem,
            smem,
            vmem,
            vmem,
            vmem,
            vmem,
            pl.BlockSpec((group, band, tile, tile), lambda u: (u, 0, 0, 0)),
            pl.BlockSpec((1, wide), lambda u: (0, u)),
        ],
        out_specs=(
            pl.BlockSpec((programs, wide), lambda u: (0, u)),
            pl.BlockSpec((JK_DEV, programs // 128, 128), lambda u: (0, 0, 0)),
            pl.BlockSpec((16, wide), lambda u: (0, u)),
        ),
        scratch_shapes=[
            pltpu.VMEM((programs, snps + 2 * reach), BF16),
            pltpu.VMEM((JK_DEV, programs, 128), F32),
        ],
        compiler_params=pltpu.CompilerParams(vmem_limit_bytes=limit),
        name="ld_scores",
    )(jk_unit, ld_scale, table, idx, lw, mix, ld_levels, snp_weight[None])

    k = ROW_CHUNKS
    half = programs // k // 2
    stages = (n // 2).bit_length() - 1
    crossed, total, sq_total = pl.pallas_call(
        functools.partial(cross_kernel, n),
        out_shape=(
            jax.ShapeDtypeStruct((JK_DEV, programs, traits), BF16),
            jax.ShapeDtypeStruct((programs, traits), BF16),
            jax.ShapeDtypeStruct((programs // 128, 128), F32),
        ),
        in_specs=[vmem] * 4,
        out_specs=(vmem,) * 3,
        scratch_shapes=[
            pltpu.VMEM((programs, traits), F32),
            pltpu.VMEM((k, half, traits), BF16),
            pltpu.VMEM((k, half, traits), BF16),
            pltpu.VMEM((k, half, traits), BF16),
            pltpu.VMEM((k, half, traits), BF16),
            pltpu.VMEM((programs // 128, 128), F32),
            pltpu.VMEM((n - 1, programs // 128, 128), F32),
            dma((k,)), dma((k,)),
            dma((k, stages)), dma((k, stages)),
            dma((k, stages)), dma((k, stages)),
            dma((k,)), dma((k,)),
            dma((n - 1,)), dma((n - 1,)),
        ],
        compiler_params=pltpu.CompilerParams(
            collective_id=1, has_side_effects=True, vmem_limit_bytes=limit
        ),
        name="cross_total",
    )(weighted, trait_z, mask, square)

    block = 128
    whole = pl.BlockSpec((JK_DEV, block, traits), lambda p: (0, p, 0))
    return pl.pallas_call(
        estimate_kernel,
        grid=(programs // block,),
        out_shape=(jax.ShapeDtypeStruct((JK_DEV, programs, traits), BF16),) * 2,
        in_specs=[whole, pl.BlockSpec((block, traits), lambda p: (p, 0)), vmem, vmem],
        out_specs=(whole, whole),
        compiler_params=pltpu.CompilerParams(vmem_limit_bytes=limit),
        name="estimates",
    )(crossed, total, square, sq_total)


def solution(mesh):
    placed = (
        P("snp", "prog"),
        P("snp", None),
        P("snp", None),
        P("snp", None, None, None),
        P("snp", None),
        P("snp"),
        P("snp", "prog"),
        P("snp", None),
    )
    return jax.shard_map(
        functools.partial(on_device, mesh.shape["snp"], mesh.shape["prog"]),
        mesh=mesh,
        in_specs=placed,
        out_specs=(P("snp", None, "prog"), P("snp", None, "prog")),
        check_vma=False,
    )
```
